512 devices in a mesh: dp: 32 (over z, x), tensor: 16 (over y, core).
Axes of the slice: x: 4, y: 8, z: 8, core: 2. Of those that a mesh axis runs over, the one named last changes fastest.
Arguments:
- features: bfloat16 [32768, 8192], P('dp', 'tensor'), may hold values from -6 to 6
- key_value_weight: bfloat16 [8192, 2048], P(None, 'tensor'), may hold values from -0.0625 to 0.0625
- adapter_down_factors: bfloat16 [8192, 16, 128], P(None, None, 'tensor'), may hold values from -0.0625 to 0.0625
- adapter_up_factors: bfloat16 [16, 128, 2048], P(None, None, 'tensor'), may hold values from -0.5 to 0.5
- row_adapter_index: int32 [32768], P('dp'), may hold values from 0 to 15, never falling along the last dimension, each value on 1 to 4096 neighbouring positions
- ranks: int32 [16], replicated, may hold values from 8 to 128, as said below
Outputs:
- projected: bfloat16 [32768, 2048], P('dp', 'tensor')
The draws below stay inside these ranges and needn't reach their ends.
Inputs may be any that keep to these rules, and one draw needn't show every extreme that they name: `ranks`: every rank is 128 // 16 times a power of two from 1 to 16; some adapter has rank 128. `row_adapter_index`: ids never fall along the rows.
All inputs are finite; a program needn't handle non-finite values.
Results may differ from the reference program's by a relative error of at most 0.0033.
Values may be sent and summed in bfloat16 or wider, within the bound.
A program may use at most 64 MiB of HBM per device.

```python
import math
import jax
import jax.numpy as jnp
import numpy as np
from jax import lax

MODEL_WIDTH = 8192
KEY_VALUE_COLS = 2048
LARGEST_RANK = 128
ADAPTER_COUNT = 16
ROWS = 32768


def draw_ranks(key, part):
    key = jax.random.fold_in(key, 7)
    first, second = jax.random.split(key)
    powers = jax.random.randint(first, (ADAPTER_COUNT,), 0, 5)
    levels = jnp.array([1, 2, 4, 8, 16], dtype=jnp.int32)
    values = LARGEST_RANK // 16 * jnp.sum(jnp.where(powers[:, None] == jnp.arange(5)[None, :], levels[None, :], 0), axis=1)
    place = jax.random.randint(second, (), 0, ADAPTER_COUNT)
    return jnp.where(jnp.arange(ADAPTER_COUNT) == place, LARGEST_RANK, values).astype(jnp.int32)


def shard_levels(stream_key, shape, pieces, least, largest):
    gain = 1.0
    for dim, shards_of in pieces:
        heights = jax.random.uniform(jax.random.fold_in(jax.random.fold_in(stream_key, 6), dim), (shards_of,), jnp.float32, least / len(pieces), largest / len(pieces))
        gain = gain * jnp.repeat(jnp.exp(heights), shape[dim] // shards_of).reshape((-1,) + (1,) * (len(shape) - 1 - dim))
    return gain


def split_up(number_of, total, most, lean):
    loads = [(1 << 20) // math.isqrt(rank ** lean) + 1 for rank in range(2, number_of + 1)]
    spare, counts = total - most - (number_of - 1), [1] * (number_of - 1)
    while spare > 0:
        movable = [i for i in range(number_of - 1) if counts[i] < most]
        mass, left = sum([loads[i] for i in movable]), spare
        for i in movable:
            more = min(most - counts[i], max(1, left * loads[i] // mass), spare)
            counts[i] = counts[i] + more
            spare = spare - more
    return np.array([most] + counts)


def ragged_sizes(key, amount, total, limit, slope):
    if amount == 2:
        one = jax.random.randint(key, (), max(1, total - limit), min(limit, total - 1) + 1)
        return jnp.stack([one, total - one])
    lengths = jnp.asarray(split_up(amount, total, limit, slope), jnp.int32)
    twos = (amount - 1) // 2
    source_of, receiver = lengths[1:1 + 2 * twos:2], lengths[2:2 + 2 * twos:2]
    room = jnp.minimum(source_of - 1, limit - receiver)
    moved = jax.random.randint(jax.random.fold_in(key, 1), (twos,), 0, 1 << 20) % (room + 1)
    lengths = lengths.at[1:1 + 2 * twos:2].set(source_of - moved).at[2:2 + 2 * twos:2].set(receiver + moved)
    return lengths[jax.random.permutation(jax.random.fold_in(key, 2), amount)]


def gaussian(key, dims, width, most, shards=(), held_as=jnp.bfloat16):
    level = shard_levels(key, dims, shards, -0.22, 0.18) if shards else 1.0
    drawn = jax.random.normal(key, dims, jnp.float32) * width * level
    return jnp.minimum(jnp.maximum(drawn, -most), most).astype(held_as)


def setup_inputs(seed: int = 0) -> dict:
    seeds = jax.random.split(jax.random.key(seed), 7)
    features = gaussian(seeds[0], (ROWS, MODEL_WIDTH), 1.0, 6.0, ((0, 32), (1, 16)))
    key_value_weight = gaussian(seeds[1], (MODEL_WIDTH, KEY_VALUE_COLS), MODEL_WIDTH ** -0.5, 0.0625, ((1, 16),))
    adapter_down_factors = gaussian(seeds[2], (MODEL_WIDTH, ADAPTER_COUNT, LARGEST_RANK), MODEL_WIDTH ** -0.5, 0.0625, ((2, 16),))
    adapter_up_factors = gaussian(seeds[3], (ADAPTER_COUNT, LARGEST_RANK, KEY_VALUE_COLS), LARGEST_RANK ** -0.5, 0.5, ((2, 16),))
    row_adapter_index = jnp.searchsorted(jnp.cumsum(ragged_sizes(seeds[4], ADAPTER_COUNT, ROWS, 2 * ROWS // ADAPTER_COUNT, 2)), jnp.arange(ROWS), side="right").astype(jnp.int32)
    ranks = draw_ranks(jax.random.fold_in(seeds[6], 71), 0)
    return dict(features=features, key_value_weight=key_value_weight, adapter_down_factors=adapter_down_factors, adapter_up_factors=adapter_up_factors, row_adapter_index=row_adapter_index, ranks=ranks)


def reference(features, key_value_weight, adapter_down_factors, adapter_up_factors, row_adapter_index, ranks):
    base = jnp.dot(features, key_value_weight, preferred_element_type=jnp.float32)
    onehot = (row_adapter_index[:, None] == jnp.arange(ADAPTER_COUNT, dtype=jnp.int32)[None, :]).astype(jnp.float32)
    row_rank = lax.optimization_barrier(jnp.sum(onehot * ranks[None, :].astype(jnp.float32), axis=1))
    intermediate_state = jnp.dot(features, adapter_down_factors.reshape(MODEL_WIDTH, ADAPTER_COUNT * LARGEST_RANK), preferred_element_type=jnp.float32)
    chosen = lax.optimization_barrier(jnp.sum(intermediate_state.reshape(-1, ADAPTER_COUNT, LARGEST_RANK) * onehot[:, :, None], axis=1))
    position = jnp.arange(LARGEST_RANK, dtype=jnp.float32)[None, :]
    low = jnp.where(position < row_rank[:, None], chosen, 0.0).astype(jnp.bfloat16)
    broadcast_rows = (low.astype(jnp.float32)[:, None, :] * onehot[:, :, None]).reshape(-1, ADAPTER_COUNT * LARGEST_RANK).astype(jnp.bfloat16)
    lowrank_update = jnp.dot(broadcast_rows, adapter_up_factors.reshape(ADAPTER_COUNT * LARGEST_RANK, KEY_VALUE_COLS), preferred_element_type=jnp.float32)
    scaled = 4.0 / jnp.sqrt(row_rank)
    return (base + scaled[:, None] * lowrank_update).astype(jnp.bfloat16)
```

```python
import functools

import jax
import jax.numpy as jnp
from jax import lax
from jax.experimental import pallas as pl
from jax.experimental.pallas import tpu as pltpu
from jax.sharding import PartitionSpec as P

MESH = pl.DeviceIdType.MESH
NX, NY, NZ, NT = 4, 8, 8, 16
ROWS = 1024
HALF = ROWS // 2
KB = 1024
KX = KB // NX
COLS = 128
ADAPTERS, RANK = 16, 128
LOWROWS = ROWS // NT
TILE = 256

OFFSETS = (4, 3, -3, 2, -2, 1, -1, 0)
OWN = 7
UP, DOWN = (0, 1, 3, 5), (0, 2, 4, 6)
LONG = (0, 1)
X_HOPS = (1, -1, 2)


def mod(value, size):
    return lax.rem(value + size, size)


def kernel(
    feat_hbm,
    weight_hbm,
    down_hbm,
    up_hbm,
    index_ref,
    ranks_ref,
    out_ref,
    feat,
    weight,
    down,
    up,
    send16,
    send32,
    recv16,
    recv32,
    row_adapter,
    row_rank,
    low_sum,
    low_send,
    low_recv,
    low,
    local_sem,
    feat_sem,
    wy_sem,
    wx_sem,
    dy_sem,
    dx_sem,
    dz_sem,
    sum_sem,
    lr_sem,
    lg_sem,
):
    g, t = lax.axis_index("dp"), lax.axis_index("tensor")
    z, x = lax.div(g, NX), lax.rem(g, NX)
    y, c = lax.div(t, 2), lax.rem(t, 2)

    def at(dz=0, dx=0, dy=0, dt=0):
        if dt:
            return (g, mod(t + dt, NT))
        return (mod(z + dz, NZ) * NX + mod(x + dx, NX), mod(y + dy, NY) * 2 + c)

    sibling = (g, y * 2 + 1 - c)

    barrier = pltpu.get_barrier_semaphore()
    for d in range(1, NT):
        pl.semaphore_signal(barrier, inc=1, device_id=at(dt=d), device_id_type=MESH)
    for d in X_HOPS:
        pl.semaphore_signal(barrier, inc=1, device_id=at(dx=d), device_id_type=MESH)
    for d in (1, -1):
        pl.semaphore_signal(barrier, inc=1, device_id=at(dz=d), device_id_type=MESH)

    def local(n, src, dst):
        return pltpu.make_async_copy(src, dst, local_sem.at[n])

    def remote(src, dst, sems, n, device):
        return pltpu.make_async_remote_copy(
            src_ref=src,
            dst_ref=dst,
            send_sem=sems.at[(0, *n)],
            recv_sem=sems.at[(1, *n)],
            device_id=device,
            device_id_type=MESH,
        )

    my_k = pl.ds(pl.multiple_of(x * KX, KX), KX)
    half_k = pl.ds(pl.multiple_of(c * (KB // 2), KB // 2), KB // 2)
    my_w = pl.ds(pl.multiple_of(y * KB + x * KX, KX), KX)
    my_d = pl.ds(pl.multiple_of(z * 16, 16), 16)
    locals_ = [
        local(0, feat_hbm, feat.at[:, half_k]),
        local(1, weight_hbm.at[my_w, :], weight.at[OWN, my_k, :]),
        local(2, down_hbm.at[my_d, my_w], down.at[z, pl.ds(pl.multiple_of(y * 16, 16), 16), my_k]),
        local(3, up_hbm, up),
    ]
    for copy in locals_:
        copy.start()

    for r in range(ROWS // 128):
        ids = index_ref[r : r + 1, :].astype(jnp.float32)
        spread = jnp.transpose(jnp.broadcast_to(ids, (128, 128)))
        row_adapter[128 * r : 128 * (r + 1), :] = spread.astype(jnp.int32)

    @pl.loop(0, ROWS // 128)
    def _(r):
        rows = pl.ds(pl.multiple_of(r * 128, 128), 128)
        ids = row_adapter[rows, :]
        rank = jnp.zeros((128, 128), jnp.float32)
        for a in range(ADAPTERS):
            rank = jnp.where(ids == a, ranks_ref[a].astype(jnp.float32), rank)
        row_rank[rows, :] = rank
        low_sum[rows, :] = jnp.zeros((128, 128), jnp.float32)

    pl.semaphore_wait(barrier, NT - 1 + len(X_HOPS) + 2)

    feat_copy = remote(feat_hbm, feat.at[:, half_k], feat_sem, (), sibling)

    def wy(i):
        to = mod(y - OFFSETS[i], NY)
        src = weight_hbm.at[pl.ds(pl.multiple_of(to * KB + x * KX, KX), KX), :]
        return remote(src, weight.at[i, my_k, :], wy_sem, (i,), at(dy=-OFFSETS[i]))

    def wx(i, n):
        part = weight.at[i, my_k, :]
        return remote(part, part, wx_sem, (i, n), at(dx=X_HOPS[n]))

    def dy(i):
        to = mod(y - OFFSETS[i], NY)
        src = down_hbm.at[my_d, pl.ds(pl.multiple_of(to * KB + x * KX, KX), KX)]
        dst = down.at[z, pl.ds(pl.multiple_of(y * 16, 16), 16), my_k]
        return remote(src, dst, dy_sem, (i,), at(dy=-OFFSETS[i]))

    def dx(n):
        part = down.at[z, :, my_k]
        return remote(part, part, dx_sem, (n,), at(dx=X_HOPS[n]))

    def dz(way, hop, q):
        sign = 1 - 2 * way
        part = down.at[mod(z - sign * hop, NZ), 64 * q : 64 * (q + 1), :]
        return remote(part, part, dz_sem, (way, hop, q), at(dz=sign))

    def rs(way, step, half):
        rows = pl.ds(half * HALF, HALF)
        src, dst = (send32, recv32) if step == 3 else (send16, recv16)
        pos = (way, rows) if step == 3 else (way, step, rows)
        return remote(
            src.at[pos], dst.at[pos], sum_sem, (way, step, half), at(dy=1 - 2 * way)
        )

    def lr(d):
        to = mod(t + d, NT)
        src = low_send.at[pl.ds(pl.multiple_of(to * LOWROWS, LOWROWS), LOWROWS), :]
        return remote(src, low_recv.at[d], lr_sem, (d,), at(dt=d))

    my_low = pl.ds(pl.multiple_of(t * LOWROWS, LOWROWS), LOWROWS)

    def lg(d):
        part = low.at[my_low, :]
        return remote(part, part, lg_sem, (d,), at(dt=d))

    sent = []

    def start(copy):
        copy.start()
        sent.append(copy)

    def tiles(half):
        return range(half * HALF, (half + 1) * HALF, TILE)

    def pass_w(i):
        if i == OWN:
            locals_[1].wait()
        else:
            wy(i).wait_recv()
        for n in range(3):
            start(wx(i, n))

    def have_w(i):
        for n in range(3):
            wx(i, n).wait_recv()

    def add_up(i, way, step, half):
        before = step >= 2 or (step == 1 and half == LONG[way])
        if before:
            rs(way, step - 1, half).wait_recv()

        @pl.loop(0, HALF // TILE)
        def _(n):
            rows = pl.ds(pl.multiple_of(half * HALF + n * TILE, TILE), TILE)
            part = jnp.dot(feat[rows, :], weight[i], preferred_element_type=jnp.float32)
            if before:
                part = part + recv16[way, step - 1, rows, :].astype(jnp.float32)
            if step == 3:
                send32[way, rows, :] = part
            else:
                send16[way, step, rows, :] = part.astype(jnp.bfloat16)

        start(rs(way, step, half))

    lane = lax.broadcasted_iota(jnp.int32, (TILE, 128), 1)
    lane_pair = lax.rem(lax.div(lane, 8), 2)

    def low_part(source):
        @pl.loop(0, ROWS // TILE)
        def _(n):
            rows = pl.ds(pl.multiple_of(n * TILE, TILE), TILE)
            part = lax.dot_general(
                feat[rows, :],
                down[source],
                (((1,), (1,)), ((), ())),
                preferred_element_type=jnp.float32,
            )
            mine = row_adapter[rows, :] == 2 * source + lane_pair
            low_sum[rows, :] = jnp.where(mine, part, low_sum[rows, :])

    def z_recv(way, hop, q):
        dz(way, hop, q).wait_recv()

    def z_forward(way, hop, q):
        z_recv(way, hop - 1, q)
        start(dz(way, hop, q))

    for i in range(7):
        start(dy(i))
    for i in range(7):
        start(wy(i))
    start(feat_copy)

    locals_[2].wait()
    for i in range(7):
        dy(i).wait_recv()
    for n in range(3):
        start(dx(n))
    pass_w(0)
    for n in range(3):
        dx(n).wait_recv()
    for q in range(2):
        for way in range(2):
            start(dz(way, 0, q))
    pass_w(1)
    pass_w(2)
    pass_w(3)
    pass_w(4)
    pass_w(5)
    pass_w(6)
    pass_w(OWN)
    locals_[0].wait()
    feat_copy.wait_recv()
    low_part(z)
    have_w(0)
    add_up(0, 0, 0, 0)
    add_up(0, 1, 0, 1)
    for way in range(2):
        z_forward(way, 1, 0)
    have_w(1)
    add_up(1, 0, 1, 1)
    add_up(1, 0, 1, 0)
    for way in range(2):
        z_forward(way, 1, 1)
    have_w(2)
    add_up(2, 1, 1, 0)
    add_up(2, 1, 1, 1)
    low_part(mod(z - 1, NZ))
    for way in range(2):
        z_forward(way, 2, 0)
    have_w(3)
    add_up(3, 0, 2, 1)
    add_up(3, 0, 2, 0)
    have_w(4)
    for way in range(2):
        z_forward(way, 2, 1)
    add_up(4, 1, 2, 0)
    add_up(4, 1, 2, 1)
    low_part(mod(z + 1, NZ))
    z_forward(0, 3, 0)
    z_recv(1, 2, 0)
    have_w(5)
    add_up(5, 0, 3, 1)
    add_up(5, 0, 3, 0)
    have_w(6)
    add_up(6, 1, 3, 0)
    add_up(6, 1, 3, 1)
    low_part(mod(z - 2, NZ))
    low_part(mod(z + 2, NZ))
    z_forward(1, 3, 1)
    z_recv(0, 2, 1)
    have_w(OWN)
    low_part(mod(z - 3, NZ))
    low_part(mod(z + 3, NZ))
    z_recv(0, 3, 0)
    z_recv(1, 3, 1)
    low_part(mod(z + 4, NZ))

    @pl.loop(0, ROWS // TILE)
    def _(n):
        rows = pl.ds(pl.multiple_of(n * TILE, TILE), TILE)
        position = lax.div(lane, 16) * 16 + c * 8 + lax.rem(lane, 8)
        kept = position.astype(jnp.float32) < row_rank[rows, :]
        mine = jnp.where(kept, low_sum[rows, :], 0.0)
        other = jnp.where(c == 0, pltpu.roll(mine, 120, 1), pltpu.roll(mine, 8, 1))
        both = jnp.where(lane_pair == c, mine + other, 0.0)
        low_send[rows, :] = both.astype(jnp.bfloat16)

    for d in range(1, NT):
        start(lr(d))
    total = low_send[my_low, :].astype(jnp.float32)
    for d in range(1, NT):
        lr(d).wait_recv()
    for d in range(1, NT):
        total = total + low_recv[d].astype(jnp.float32)
    low[my_low, :] = total.astype(jnp.bfloat16)
    for d in range(1, NT):
        start(lg(d))

    for way in range(2):
        for half in range(2):
            rs(way, 3, half).wait_recv()

    @pl.loop(0, ROWS // TILE)
    def _(n):
        rows = pl.ds(pl.multiple_of(n * TILE, TILE), TILE)
        part = jnp.dot(feat[rows, :], weight[OWN], preferred_element_type=jnp.float32)
        recv32[0, rows, :] = part + (recv32[0, rows, :] + recv32[1, rows, :])

    locals_[3].wait()
    for d in range(1, NT):
        lg(d).wait_recv()

    @pl.loop(0, ROWS // TILE)
    def _(n):
        rows = pl.ds(pl.multiple_of(n * TILE, TILE), TILE)
        code = low[rows, :].astype(jnp.float32)
        ids = row_adapter[rows, :]
        spread = [
            jnp.where(ids == a, code, 0.0).astype(jnp.bfloat16) for a in range(ADAPTERS)
        ]
        update = jnp.dot(
            jnp.concatenate(spread, axis=1), up[...], preferred_element_type=jnp.float32
        )
        scale = 4.0 / jnp.sqrt(row_rank[rows, :])
        out_ref[rows, :] = (recv32[0, rows, :] + scale * update).astype(jnp.bfloat16)

    for copy in sent:
        copy.wait_send()


def body(features, key_value_weight, adapter_down_factors, adapter_up_factors, row_adapter_index, ranks):
    down = adapter_down_factors.transpose(1, 2, 0).reshape(ADAPTERS * 8, NY * KB)
    up = adapter_up_factors.reshape(ADAPTERS * RANK, COLS)
    index = row_adapter_index.reshape(ROWS // 128, 128)
    vmem, any_ = pl.BlockSpec(memory_space=pltpu.VMEM), pl.BlockSpec(memory_space=pl.ANY)
    bf16, f32 = jnp.bfloat16, jnp.float32
    dma = pltpu.SemaphoreType.DMA
    return pl.pallas_call(
        kernel,
        out_shape=jax.ShapeDtypeStruct((ROWS, COLS), bf16),
        in_specs=[any_, any_, any_, any_, vmem, pl.BlockSpec(memory_space=pltpu.SMEM)],
        out_specs=vmem,
        scratch_shapes=[
            pltpu.VMEM((ROWS, KB), bf16),
            pltpu.VMEM((NY, KB, COLS), bf16),
            pltpu.VMEM((NZ, NY * 16, KB), bf16),
            pltpu.VMEM((ADAPTERS * RANK, COLS), bf16),
            pltpu.VMEM((2, 3, ROWS, COLS), bf16),
            pltpu.VMEM((2, ROWS, COLS), f32),
            pltpu.VMEM((2, 3, ROWS, COLS), bf16),
            pltpu.VMEM((2, ROWS, COLS), f32),
            pltpu.VMEM((ROWS, 128), jnp.int32),
            pltpu.VMEM((ROWS, 128), f32),
            pltpu.VMEM((ROWS, 128), f32),
            pltpu.VMEM((ROWS, 128), bf16),
            pltpu.VMEM((NT, LOWROWS, 128), bf16),
            pltpu.VMEM((ROWS, 128), bf16),
            dma((4,)),
            dma((2,)),
            dma((2, 7)),
            dma((2, 8, 3)),
            dma((2, 7)),
            dma((2, 3)),
            dma((2, 2, 4, 2)),
            dma((2, 2, 4, 2)),
            dma((2, NT)),
            dma((2, NT)),
        ],
        compiler_params=pltpu.CompilerParams(
            collective_id=0, has_side_effects=True, vmem_limit_bytes=40 << 20
        ),
        cost_estimate=pl.CostEstimate(
            flops=2 * ROWS * KB * 2048 + 2 * ROWS * 2048 * COLS,
            bytes_accessed=8 << 20,
            transcendentals=0,
        ),
    )(features, key_value_weight, down, up, index, ranks)


def solution(mesh):
    in_specs = (
        P("dp", "tensor"),
        P(None, "tensor"),
        P(None, None, "tensor"),
        P(None, None, "tensor"),
        P("dp"),
        P(),
    )
    out_specs = P("dp", "tensor")
    return jax.shard_map(body, mesh=mesh, in_specs=in_specs, out_specs=out_specs, check_vma=False)
```

```python
import functools

import jax
import jax.numpy as jnp
from jax import lax
from jax.experimental import pallas as pl
from jax.experimental.pallas import tpu as pltpu
from jax.sharding import PartitionSpec as P

MESH = pl.DeviceIdType.MESH
NX, NY, NZ, NT = 4, 8, 8, 16
ROWS = 1024
HALF = ROWS // 2
KB = 1024
KX = KB // NX
COLS = 128
ADAPTERS, RANK = 16, 128
LOWROWS = ROWS // NT
PAIR = LOWROWS // 2
TILE = 256

OFFSETS = (4, 3, -3, 2, -2, 1, -1)
UP, DOWN = (0, 1, 3, 5), (0, 2, 4, 6)
LONG = (0, 1)
X_HOPS = (1, -1, 2)


def mod(value, size):
    return lax.rem(value + size, size)


def kernel(
    feat_hbm,
    weight_hbm,
    down_hbm,
    up_hbm,
    index_hbm,
    ranks_hbm,
    out_ref,
    feat,
    weight,
    own_weight,
    down,
    up,
    index_ref,
    ranks_ref,
    send16,
    send32,
    recv16,
    recv32,
    row_adapter,
    row_rank,
    low_sum,
    low_send,
    low_recv,
    low,
    base,
    local_sem,
    feat_sem,
    wy_sem,
    wx_sem,
    dy_sem,
    dx_sem,
    dz_sem,
    sum_sem,
    lr_sem,
    lg_sem,
    lh_sem,
):
    g, t = lax.axis_index("dp"), lax.axis_index("tensor")
    z, x = lax.div(g, NX), lax.rem(g, NX)
    y, c = lax.div(t, 2), lax.rem(t, 2)

    def at(dz=0, dx=0, dy=0):
        return (mod(z + dz, NZ) * NX + mod(x + dx, NX), mod(y + dy, NY) * 2 + c)

    def line(n):
        return (g, mod(y + n // 2, NY) * 2 + (c if n % 2 == 0 else 1 - c))

    sibling = line(1)

    barrier = pltpu.get_barrier_semaphore()
    for n in range(1, NT):
        pl.semaphore_signal(barrier, inc=1, device_id=line(n), device_id_type=MESH)
    for d in X_HOPS:
        pl.semaphore_signal(barrier, inc=1, device_id=at(dx=d), device_id_type=MESH)
    for d in (1, -1):
        pl.semaphore_signal(barrier, inc=1, device_id=at(dz=d), device_id_type=MESH)

    def local(n, src, dst):
        return pltpu.make_async_copy(src, dst, local_sem.at[n])

    def remote(src, dst, sems, n, device):
        return pltpu.make_async_remote_copy(
            src_ref=src,
            dst_ref=dst,
            send_sem=sems.at[(0, *n)],
            recv_sem=sems.at[(1, *n)],
            device_id=device,
            device_id_type=MESH,
        )

    my_k = pl.ds(pl.multiple_of(x * KX, KX), KX)
    half_k = pl.ds(pl.multiple_of(c * (KB // 2), KB // 2), KB // 2)
    chip_k = pl.ds(pl.multiple_of(y * KB, KB), KB)

    def down_k(chip, k):
        return pl.ds(pl.multiple_of(chip * KB + k * 128, 128), 128)

    own_rows, other_rows = pl.ds(0, 16), pl.ds(16, NY * 16 - 16)
    locals_ = [
        local(0, feat_hbm, feat.at[:, half_k]),
        local(1, weight_hbm.at[chip_k, :], own_weight),
        local(2, up_hbm, up),
        local(3, index_hbm, index_ref),
        local(4, ranks_hbm, ranks_ref),
        *[
            local(5 + k, down_hbm.at[:, :, down_k(y, k)], down.at[k, :, own_rows])
            for k in range(KB // 128)
        ],
    ]
    for copy in locals_:
        copy.start()

    pl.semaphore_wait(barrier, NT - 1 + len(X_HOPS) + 2)

    feat_copy = remote(feat_hbm, feat.at[:, half_k], feat_sem, (), sibling)

    def wy(i):
        to = mod(y - OFFSETS[i], NY)
        src = weight_hbm.at[pl.ds(pl.multiple_of(to * KB + x * KX, KX), KX), :]
        return remote(src, weight.at[i, my_k, :], wy_sem, (i,), at(dy=-OFFSETS[i]))

    def wx(i, n):
        part = weight.at[i, my_k, :]
        return remote(part, part, wx_sem, (i, n), at(dx=X_HOPS[n]))

    def dy(i, h):
        to = mod(y - OFFSETS[i], NY)
        src = down_hbm.at[z, :, down_k(to, 2 * x + h)]
        dst = down.at[2 * x + h, z, pl.ds(OFFSETS[i] % NY * 16, 16)]
        return remote(src, dst, dy_sem, (i, h), at(dy=-OFFSETS[i]))

    def dx(n):
        part = down.at[pl.ds(2 * x, 2), z, other_rows]
        return remote(part, part, dx_sem, (n,), at(dx=X_HOPS[n]))

    def dz(way, hop, part):
        sign = 1 - 2 * way
        of = mod(x + (0, -1, 1, 2)[part], NX)
        ref = down.at[pl.ds(2 * of, 2), mod(z - sign * hop, NZ), other_rows]
        return remote(ref, ref, dz_sem, (way, hop, part), at(dz=sign))

    def rs(way, step, half):
        if step == 3 and half == LONG[way]:
            src, dst = send32.at[way], recv32.at[way]
        else:
            rows = pl.ds(half * HALF, HALF)
            src, dst = send16.at[way, step, rows], recv16.at[way, step, rows]
        return remote(src, dst, sum_sem, (way, step, half), at(dy=1 - 2 * way))

    def lr(n):
        to = mod(y + n // 2, NY), c if n % 2 == 0 else 1 - c
        return remote(low_send.at[to], low_recv.at[n], lr_sem, (n,), line(n))

    def lg(d):
        part = low.at[y, c]
        return remote(part, part, lg_sem, (d,), at(dy=d))

    def lh():
        part = low.at[:, c]
        return remote(part, part, lh_sem, (), sibling)

    sent, late = [], []

    def start(copy, among=sent):
        copy.start()
        among.append(copy)

    def drain(copies):
        for copy in copies:
            copy.wait_send()
        copies.clear()

    def pass_w(i):
        wy(i).wait_recv()
        for n in (2, 0, 1):
            start(wx(i, n))

    def have_w(i):
        for n in range(3):
            wx(i, n).wait_recv()

    def add_up(i, way, step, half):
        before = step >= 2 or (step == 1 and half == LONG[way])
        if before:
            rs(way, step - 1, half).wait_recv()

        @pl.loop(0, HALF // TILE)
        def _(n):
            rows = pl.ds(pl.multiple_of(half * HALF + n * TILE, TILE), TILE)
            part = jnp.dot(feat[rows, :], weight[i], preferred_element_type=jnp.float32)
            if before:
                part = part + recv16[way, step - 1, rows, :].astype(jnp.float32)
            if step == 3 and half == LONG[way]:
                send32[way, pl.ds(pl.multiple_of(n * TILE, TILE), TILE), :] = part
            else:
                send16[way, step, rows, :] = part.astype(jnp.bfloat16)

        start(rs(way, step, half), late if step == 3 else sent)

    lane = lax.broadcasted_iota(jnp.int32, (TILE, 128), 1)
    lane_pair = lax.rem(lax.div(lane, 8), 2)
    pair_lane = lax.rem(
        lax.div(lax.broadcasted_iota(jnp.int32, (TILE // 128, 2, PAIR, 128), 3), 8), 2
    )

    def tile_of(ref, n):
        return ref[pl.ds(n * (TILE // 128), TILE // 128)].reshape(TILE, 128)

    def low_part(back, other_back):
        first, second = mod(z - back, NZ), mod(z - other_back, NZ)
        factors = jnp.concatenate(
            [
                jnp.concatenate([down[k, source] for k in range(KB // 128)], axis=1)
                for source in (first, second)
            ],
            axis=0,
        )

        @pl.loop(0, ROWS // TILE)
        def _(n):
            rows = pl.ds(pl.multiple_of(n * TILE, TILE), TILE)
            part = lax.dot_general(
                feat[rows, :],
                factors,
                (((1,), (1,)), ((), ())),
                preferred_element_type=jnp.float32,
            )
            ids = tile_of(row_adapter, n)
            total = low_sum[rows, :]
            for source, columns in ((first, part[:, :128]), (second, part[:, 128:])):
                total = jnp.where(ids == 2 * source + lane_pair, columns, total)
            low_sum[rows, :] = total

    def z_got(way, hop, part):
        dz(way, hop, part).wait_recv()
        if hop < 2 or (hop == 2 and part in ((0, 1), (2, 3))[way]):
            start(dz(way, hop + 1, part))

    def low_codes():
        @pl.loop(0, ROWS // TILE)
        def _(n):
            rows = pl.ds(pl.multiple_of(n * TILE, TILE), TILE)
            mine = pltpu.roll(low_sum[rows, :], 16 * y, 1)
            position = lax.div(lane, 16) * 16 + c * 8 + lax.rem(lane, 8)
            kept = position.astype(jnp.float32) < tile_of(row_rank, n)
            mine = jnp.where(kept, mine, 0.0)
            across = jnp.where(lane_pair == 0, pltpu.roll(mine, 120, 1), pltpu.roll(mine, 8, 1))
            both = (mine + across).reshape(TILE // 128, 2, 2, PAIR, 128)
            pair = jnp.where(pair_lane == 0, both[:, :, 0], both[:, :, 1])
            low_send[pl.ds(n * (TILE // 128), TILE // 128)] = pair.astype(jnp.bfloat16)

        drain(sent)
        for n in range(1, NT):
            start(lr(n))

    def low_total():
        totals = [low_send[y, c].astype(jnp.float32), None]
        for n in range(1, NT):
            lr(n).wait_recv()
        for n in range(1, NT):
            part = low_recv[n].astype(jnp.float32)
            totals[n % 2] = part if totals[n % 2] is None else totals[n % 2] + part
        even = jnp.where(c == 0, totals[0], totals[1])
        odd = jnp.where(c == 0, totals[1], totals[0])
        first = jnp.where(lane_pair[:PAIR] == 0, even, pltpu.roll(odd, 8, 1))
        second = jnp.where(lane_pair[:PAIR] == 0, pltpu.roll(even, 120, 1), odd)
        low[y, c, :PAIR] = first.astype(jnp.bfloat16)
        low[y, c, PAIR:] = second.astype(jnp.bfloat16)
        drain(sent)
        for d in range(1, NY):
            start(lg(d))

    def own_part():
        locals_[1].wait()

        @pl.loop(0, ROWS // TILE)
        def _(n):
            rows = pl.ds(pl.multiple_of(n * TILE, TILE), TILE)
            part = jnp.dot(feat[rows, :], own_weight[...], preferred_element_type=jnp.float32)
            base[pl.ds(n * (TILE // 128), TILE // 128)] = part.reshape(TILE // 128, 2, LOWROWS, 128)

    def all_parts():
        for way in range(2):
            for half in range(2):
                rs(way, 3, half).wait_recv()
        for half in range(2):
            rows = slice(half * HALF, (half + 1) * HALF)
            chips = slice(half * NY // 2, (half + 1) * NY // 2)
            total = base[chips]
            for way in range(2):
                if half == LONG[way]:
                    total += recv32[way].reshape(total.shape)
                else:
                    total += recv16[way, 3, rows, :].astype(jnp.float32).reshape(total.shape)
            base[chips] = total
        drain(late)

    def finish(core):
        @pl.loop(0, NY * LOWROWS // TILE)
        def _(n):
            group = (pl.ds(n * (TILE // LOWROWS), TILE // LOWROWS), core)
            code = low[group].reshape(TILE, 128).astype(jnp.float32)
            ids = row_adapter[group].reshape(TILE, 128)
            spread = [
                jnp.where(ids == a, code, 0.0).astype(jnp.bfloat16) for a in range(ADAPTERS)
            ]
            update = jnp.dot(
                jnp.concatenate(spread, axis=1), up[...], preferred_element_type=jnp.float32
            )
            scale = 4.0 / jnp.sqrt(row_rank[group])
            total = base[group] + scale * update.reshape(scale.shape)
            out_ref[group] = total.astype(jnp.bfloat16)

    for i in range(7):
        for h in range(2):
            start(dy(i, h))
    for i in range(7):
        start(wy(i))
    start(feat_copy)
    locals_[3].wait()
    locals_[4].wait()
    for r in range(ROWS // 128):
        ids = index_ref[r : r + 1, :].astype(jnp.float32)
        spread = jnp.transpose(jnp.broadcast_to(ids, (128, 128)))
        row_adapter[r] = spread.astype(jnp.int32).reshape(2, LOWROWS, 128)

    @pl.loop(0, ROWS // 128)
    def _(r):
        ids = row_adapter[r]
        rank = jnp.zeros((2, LOWROWS, 128), jnp.float32)
        for a in range(ADAPTERS):
            rank = jnp.where(ids == a, ranks_ref[a].astype(jnp.float32), rank)
        row_rank[r] = rank

    low_sum[...] = jnp.zeros_like(low_sum)
    for i in range(7):
        for h in range(2):
            dy(i, h).wait_recv()
    for n in (2, 0, 1):
        start(dx(n))
    for way in range(2):
        start(dz(way, 0, 0))
    locals_[0].wait()
    feat_copy.wait_recv()
    own_part()
    pass_w(0)
    z_got(0, 0, 0)
    z_got(1, 0, 0)
    for n in range(3):
        dx(n).wait_recv()
    for part in (1, 2, 3):
        for way in range(2):
            start(dz(way, 0, part))
    pass_w(1)
    pass_w(2)
    z_got(0, 1, 0)
    z_got(1, 1, 0)
    pass_w(3)
    z_got(0, 0, 1)
    z_got(1, 0, 1)
    pass_w(4)
    pass_w(5)
    pass_w(6)
    z_got(0, 0, 2)
    z_got(1, 0, 2)
    have_w(0)
    add_up(0, 0, 0, 0)
    add_up(0, 1, 0, 1)
    z_got(0, 0, 3)
    z_got(1, 0, 3)
    have_w(1)
    add_up(1, 0, 1, 1)
    z_got(0, 2, 0)
    z_got(1, 2, 0)
    for k in range(KB // 128):
        locals_[5 + k].wait()
    low_part(0, 1)
    z_got(0, 1, 1)
    z_got(1, 1, 1)
    have_w(2)
    add_up(2, 1, 1, 0)
    z_got(0, 1, 2)
    z_got(1, 1, 2)
    add_up(1, 0, 1, 0)
    add_up(2, 1, 1, 1)
    z_got(0, 1, 3)
    z_got(1, 1, 3)
    have_w(3)
    low_part(7, 2)
    z_got(0, 3, 0)
    z_got(1, 2, 1)
    add_up(3, 0, 2, 1)
    z_got(0, 2, 1)
    z_got(1, 2, 2)
    have_w(4)
    add_up(4, 1, 2, 0)
    z_got(0, 2, 2)
    z_got(1, 2, 3)
    add_up(3, 0, 2, 0)
    have_w(5)
    z_got(0, 2, 3)
    low_part(6, 3)
    z_got(0, 3, 1)
    z_got(1, 3, 2)
    add_up(4, 1, 2, 1)
    z_got(1, 3, 3)
    have_w(6)
    add_up(5, 0, 3, 1)
    add_up(6, 1, 3, 0)
    low_part(5, 4)
    low_codes()
    add_up(5, 0, 3, 0)
    add_up(6, 1, 3, 1)
    low_total()
    all_parts()
    for d in range(1, NY):
        lg(d).wait_recv()
    start(lh())
    locals_[2].wait()
    finish(c)
    lh().wait_recv()
    finish(1 - c)
    drain(sent)


def body(features, key_value_weight, adapter_down_factors, adapter_up_factors, row_adapter_index, ranks):
    down = adapter_down_factors.transpose(1, 2, 0).reshape(NZ, 16, NY * KB)
    up = adapter_up_factors.reshape(ADAPTERS * RANK, COLS)
    index = row_adapter_index.reshape(ROWS // 128, 128)
    vmem, any_ = pl.BlockSpec(memory_space=pltpu.VMEM), pl.BlockSpec(memory_space=pl.ANY)
    bf16, f32 = jnp.bfloat16, jnp.float32
    dma = pltpu.SemaphoreType.DMA
    return pl.pallas_call(
        kernel,
        out_shape=jax.ShapeDtypeStruct((NY, 2, LOWROWS, COLS), bf16),
        in_specs=[any_] * 6,
        out_specs=vmem,
        scratch_shapes=[
            pltpu.VMEM((ROWS, KB), bf16),
            pltpu.VMEM((NY - 1, KB, COLS), bf16),
            pltpu.VMEM((KB, COLS), bf16),
            pltpu.VMEM((KB // 128, NZ, NY * 16, 128), bf16),
            pltpu.VMEM((ADAPTERS * RANK, COLS), bf16),
            pltpu.VMEM((ROWS // 128, 128), jnp.int32),
            pltpu.SMEM((ADAPTERS,), jnp.int32),
            pltpu.VMEM((2, 4, ROWS, COLS), bf16),
            pltpu.VMEM((2, HALF, COLS), f32),
            pltpu.VMEM((2, 4, ROWS, COLS), bf16),
            pltpu.VMEM((2, HALF, COLS), f32),
            pltpu.VMEM((NY, 2, LOWROWS, 128), jnp.int32),
            pltpu.VMEM((NY, 2, LOWROWS, 128), f32),
            pltpu.VMEM((ROWS, 128), f32),
            pltpu.VMEM((NY, 2, PAIR, 128), bf16),
            pltpu.VMEM((NT, PAIR, 128), bf16),
            pltpu.VMEM((NY, 2, LOWROWS, 128), bf16),
            pltpu.VMEM((NY, 2, LOWROWS, COLS), f32),
            dma((5 + KB // 128,)),
            dma((2,)),
            dma((2, 7)),
            dma((2, 7, 3)),
            dma((2, 7, 2)),
            dma((2, 3)),
            dma((2, 2, 4, 4)),
            dma((2, 2, 4, 2)),
            dma((2, NT)),
            dma((2, NY)),
            dma((2,)),
        ],
        compiler_params=pltpu.CompilerParams(
            collective_id=0, has_side_effects=True, vmem_limit_bytes=60 << 20
        ),
        cost_estimate=pl.CostEstimate(
            flops=2 * ROWS * KB * 2048 + 2 * ROWS * 2048 * COLS,
            bytes_accessed=8 << 20,
            transcendentals=0,
        ),
    )(features, key_value_weight, down, up, index, ranks).reshape(ROWS, COLS)


def solution(mesh):
    in_specs = (
        P("dp", "tensor"),
        P(None, "tensor"),
        P(None, None, "tensor"),
        P(None, None, "tensor"),
        P("dp"),
        P(),
    )
    out_specs = P("dp", "tensor")
    return jax.shard_map(body, mesh=mesh, in_specs=in_specs, out_specs=out_specs, check_vma=False)
```

```python
import functools

import jax
import jax.numpy as jnp
from jax import lax
from jax.experimental import pallas as pl
from jax.experimental.pallas import tpu as pltpu
from jax.sharding import PartitionSpec as P

MESH = pl.DeviceIdType.MESH
NX, NY, NZ, NT = 4, 8, 8, 16
ROWS = 1024
HALF = ROWS // 2
KB = 1024
KX = KB // NX
COLS = 128
ADAPTERS, RANK = 16, 128
LOWROWS = ROWS // NT
PAIR = LOWROWS // 2
TILE = 256

OFFSETS = (4, 3, -3, 2, -2, 1, -1)
UP, DOWN = (0, 1, 3, 5), (0, 2, 4, 6)
LONG = (0, 1)
X_HOPS = (1, -1, 2)


def mod(value, size):
    return lax.rem(value + size, size)


def kernel(
    feat_hbm,
    weight_hbm,
    down_hbm,
    up_hbm,
    index_hbm,
    ranks_hbm,
    out_ref,
    feat,
    weight,
    own_weight,
    down,
    up,
    index_ref,
    ranks_ref,
    send16,
    send32,
    recv16,
    recv32,
    row_adapter,
    row_rank,
    low_sum,
    low_send,
    low_recv,
    low,
    base,
    local_sem,
    feat_sem,
    wy_sem,
    wx_sem,
    dy_sem,
    dx_sem,
    dz_sem,
    sum_sem,
    lr_sem,
    lg_sem,
    lh_sem,
):
    g, t = lax.axis_index("dp"), lax.axis_index("tensor")
    z, x = lax.div(g, NX), lax.rem(g, NX)
    y, c = lax.div(t, 2), lax.rem(t, 2)

    def at(dz=0, dx=0, dy=0):
        return (mod(z + dz, NZ) * NX + mod(x + dx, NX), mod(y + dy, NY) * 2 + c)

    def line(n):
        return (g, mod(y + n // 2, NY) * 2 + (c if n % 2 == 0 else 1 - c))

    sibling = line(1)

    barrier = pltpu.get_barrier_semaphore()
    for n in range(1, NT):
        pl.semaphore_signal(barrier, inc=1, device_id=line(n), device_id_type=MESH)
    for d in X_HOPS:
        pl.semaphore_signal(barrier, inc=1, device_id=at(dx=d), device_id_type=MESH)
    for d in (1, -1):
        pl.semaphore_signal(barrier, inc=1, device_id=at(dz=d), device_id_type=MESH)

    def local(n, src, dst):
        return pltpu.make_async_copy(src, dst, local_sem.at[n])

    def remote(src, dst, sems, n, device):
        return pltpu.make_async_remote_copy(
            src_ref=src,
            dst_ref=dst,
            send_sem=sems.at[(0, *n)],
            recv_sem=sems.at[(1, *n)],
            device_id=device,
            device_id_type=MESH,
        )

    my_k = pl.ds(pl.multiple_of(x * KX, KX), KX)
    half_k = pl.ds(pl.multiple_of(c * (KB // 2), KB // 2), KB // 2)
    chip_k = pl.ds(pl.multiple_of(y * KB, KB), KB)

    def down_k(chip, k):
        return pl.ds(pl.multiple_of(chip * KB + k * 128, 128), 128)

    own_rows, other_rows = pl.ds(0, 16), pl.ds(16, NY * 16 - 16)
    locals_ = [
        local(0, feat_hbm, feat.at[:, half_k]),
        local(1, weight_hbm.at[chip_k, :], own_weight),
        local(2, up_hbm, up),
        local(3, index_hbm, index_ref),
        local(4, ranks_hbm, ranks_ref),
        *[
            local(5 + k, down_hbm.at[:, :, down_k(y, k)], down.at[k, :, own_rows])
            for k in range(KB // 128)
        ],
    ]
    for copy in locals_[3:5]:
        copy.start()

    pl.semaphore_wait(barrier, NT - 1 + len(X_HOPS) + 2)

    feat_copy = remote(feat_hbm, feat.at[:, half_k], feat_sem, (), sibling)

    def wy(i):
        to = mod(y - OFFSETS[i], NY)
        src = weight_hbm.at[pl.ds(pl.multiple_of(to * KB + x * KX, KX), KX), :]
        return remote(src, weight.at[i, my_k, :], wy_sem, (i,), at(dy=-OFFSETS[i]))

    def wx(i, n):
        part = weight.at[i, my_k, :]
        return remote(part, part, wx_sem, (i, n), at(dx=X_HOPS[n]))

    def dy(i, h):
        to = mod(y - OFFSETS[i], NY)
        src = down_hbm.at[z, :, down_k(to, 2 * x + h)]
        dst = down.at[2 * x + h, z, pl.ds(OFFSETS[i] % NY * 16, 16)]
        return remote(src, dst, dy_sem, (i, h), at(dy=-OFFSETS[i]))

    def dx(n):
        part = down.at[pl.ds(2 * x, 2), z, other_rows]
        return remote(part, part, dx_sem, (n,), at(dx=X_HOPS[n]))

    def dz(way, hop, part):
        sign = 1 - 2 * way
        of = mod(x + (0, -1, 1, 2)[part], NX)
        ref = down.at[pl.ds(2 * of, 2), mod(z - sign * hop, NZ), other_rows]
        return remote(ref, ref, dz_sem, (way, hop, part), at(dz=sign))

    def rs(way, step, half):
        if step == 3 and half == LONG[way]:
            src, dst = send32.at[way], recv32.at[way]
        else:
            rows = pl.ds(half * HALF, HALF)
            src, dst = send16.at[way, step, rows], recv16.at[way, step, rows]
        return remote(src, dst, sum_sem, (way, step, half), at(dy=1 - 2 * way))

    def lr(n):
        to = mod(y + n // 2, NY), c if n % 2 == 0 else 1 - c
        return remote(low_send.at[to], low_recv.at[n], lr_sem, (n,), line(n))

    def lg(d):
        part = low.at[y, c]
        return remote(part, part, lg_sem, (d,), at(dy=d))

    def lh():
        part = low.at[:, c]
        return remote(part, part, lh_sem, (), sibling)

    sent, late, codes = [], [], []

    def start(copy, among=sent):
        copy.start()
        among.append(copy)

    def drain(copies):
        for copy in copies:
            copy.wait_send()
        copies.clear()

    def pass_w(i):
        wy(i).wait_recv()
        for n in (2, 0, 1):
            start(wx(i, n))

    def have_w(i):
        for n in range(3):
            wx(i, n).wait_recv()

    def add_up(i, way, step, half):
        before = step >= 2 or (step == 1 and half == LONG[way])
        if before:
            rs(way, step - 1, half).wait_recv()

        @pl.loop(0, HALF // TILE)
        def _(n):
            rows = pl.ds(pl.multiple_of(half * HALF + n * TILE, TILE), TILE)
            part = jnp.dot(feat[rows, :], weight[i], preferred_element_type=jnp.float32)
            if before:
                part = part + recv16[way, step - 1, rows, :].astype(jnp.float32)
            if step == 3 and half == LONG[way]:
                send32[way, pl.ds(pl.multiple_of(n * TILE, TILE), TILE), :] = part
            else:
                send16[way, step, rows, :] = part.astype(jnp.bfloat16)

        start(rs(way, step, half), late if step == 3 else sent)

    lane = lax.broadcasted_iota(jnp.int32, (TILE, 128), 1)
    lane_pair = lax.rem(lax.div(lane, 8), 2)
    pair_lane = lax.rem(
        lax.div(lax.broadcasted_iota(jnp.int32, (2, PAIR, 128), 2), 8), 2
    )

    def tile_of(ref, n):
        return ref[pl.ds(n * (TILE // 128), TILE // 128)].reshape(TILE, 128)

    def low_part(back, other_back):
        first, second = mod(z - back, NZ), mod(z - other_back, NZ)
        factors = jnp.concatenate(
            [
                jnp.concatenate([down[k, source] for k in range(KB // 128)], axis=1)
                for source in (first, second)
            ],
            axis=0,
        )

        @pl.loop(0, ROWS // TILE)
        def _(n):
            rows = pl.ds(pl.multiple_of(n * TILE, TILE), TILE)
            part = lax.dot_general(
                feat[rows, :],
                factors,
                (((1,), (1,)), ((), ())),
                preferred_element_type=jnp.float32,
            )
            ids = tile_of(row_adapter, n)
            total = low_sum[rows, :]
            for source, columns in ((first, part[:, :128]), (second, part[:, 128:])):
                total = jnp.where(ids == 2 * source + lane_pair, columns, total)
            low_sum[rows, :] = total

    def z_got(way, hop, part):
        dz(way, hop, part).wait_recv()
        if hop < 2 or (hop == 2 and part in ((0, 1), (2, 3))[way]):
            start(dz(way, hop + 1, part))

    def low_codes():
        position = lax.div(lane, 16) * 16 + c * 8 + lax.rem(lane, 8)
        for d in (4, 3, 5, 2, 6, 1, 7, 0):
            chip = mod(y + d, NY)
            rows = pl.ds(pl.multiple_of(chip * 128, 128), 128)
            mine = pltpu.roll(low_sum[rows, :], 16 * y, 1)
            kept = position[:128].astype(jnp.float32) < row_rank[chip].reshape(128, 128)
            mine = jnp.where(kept, mine, 0.0)
            left, right = pltpu.roll(mine, 120, 1), pltpu.roll(mine, 8, 1)
            both = mine + jnp.where(lane_pair[:128] == 0, left, right)
            both = both.reshape(2, 2, PAIR, 128)
            pair = jnp.where(pair_lane == 0, both[:, 0], both[:, 1])
            low_send[chip] = pair.astype(jnp.bfloat16)
            for n in (2 * d, 2 * d + 1):
                if n:
                    start(lr(n), codes)
        drain(sent)

    def low_total():
        totals = [low_send[y, c].astype(jnp.float32), None]
        for n in range(1, NT):
            lr(n).wait_recv()
        for n in range(1, NT):
            part = low_recv[n].astype(jnp.float32)
            totals[n % 2] = part if totals[n % 2] is None else totals[n % 2] + part
        even = jnp.where(c == 0, totals[0], totals[1])
        odd = jnp.where(c == 0, totals[1], totals[0])
        first = jnp.where(lane_pair[:PAIR] == 0, even, pltpu.roll(odd, 8, 1))
        second = jnp.where(lane_pair[:PAIR] == 0, pltpu.roll(even, 120, 1), odd)
        low[y, c, :PAIR] = first.astype(jnp.bfloat16)
        low[y, c, PAIR:] = second.astype(jnp.bfloat16)
        for d in range(1, NY):
            start(lg(d))
        drain(codes)

    def own_part():
        locals_[1].wait()

        @pl.loop(0, ROWS // TILE)
        def _(n):
            rows = pl.ds(pl.multiple_of(n * TILE, TILE), TILE)
            part = jnp.dot(feat[rows, :], own_weight[...], preferred_element_type=jnp.float32)
            base[pl.ds(n * (TILE // 128), TILE // 128)] = part.reshape(TILE // 128, 2, LOWROWS, 128)

    def all_parts():
        for way in range(2):
            for half in range(2):
                rs(way, 3, half).wait_recv()
        for half in range(2):
            rows = slice(half * HALF, (half + 1) * HALF)
            chips = slice(half * NY // 2, (half + 1) * NY // 2)
            total = base[chips]
            for way in range(2):
                if half == LONG[way]:
                    total += recv32[way].reshape(total.shape)
                else:
                    total += recv16[way, 3, rows, :].astype(jnp.float32).reshape(total.shape)
            base[chips] = total
        drain(late)

    def finish(core):
        @pl.loop(0, NY * LOWROWS // TILE)
        def _(n):
            group = (pl.ds(n * (TILE // LOWROWS), TILE // LOWROWS), core)
            code = low[group].reshape(TILE, 128).astype(jnp.float32)
            ids = row_adapter[group].reshape(TILE, 128)
            spread = [
                jnp.where(ids == a, code, 0.0).astype(jnp.bfloat16) for a in range(ADAPTERS)
            ]
            update = jnp.dot(
                jnp.concatenate(spread, axis=1), up[...], preferred_element_type=jnp.float32
            )
            scale = 4.0 / jnp.sqrt(row_rank[group])
            total = base[group] + scale * update.reshape(scale.shape)
            out_ref[group] = total.astype(jnp.bfloat16)

    for i in range(7):
        for h in range(2):
            start(dy(i, h))
    for i in range(7):
        start(wy(i))
    start(feat_copy)
    for copy in locals_[:3] + locals_[5:]:
        copy.start()
    locals_[3].wait()
    locals_[4].wait()
    for r in range(ROWS // 128):
        ids = index_ref[r : r + 1, :].astype(jnp.float32)
        spread = jnp.transpose(jnp.broadcast_to(ids, (128, 128)))
        row_adapter[r] = spread.astype(jnp.int32).reshape(2, LOWROWS, 128)

    @pl.loop(0, ROWS // 128)
    def _(r):
        ids = row_adapter[r]
        rank = jnp.zeros((2, LOWROWS, 128), jnp.float32)
        for a in range(ADAPTERS):
            rank = jnp.where(ids == a, ranks_ref[a].astype(jnp.float32), rank)
        row_rank[r] = rank

    low_sum[...] = jnp.zeros_like(low_sum)
    for i in range(7):
        for h in range(2):
            dy(i, h).wait_recv()
    for n in (2, 0, 1):
        start(dx(n))
    for way in range(2):
        start(dz(way, 0, 0))
    locals_[0].wait()
    feat_copy.wait_recv()
    own_part()
    pass_w(0)
    z_got(0, 0, 0)
    z_got(1, 0, 0)
    for n in range(3):
        dx(n).wait_recv()
    for part in (1, 2, 3):
        for way in range(2):
            start(dz(way, 0, part))
    pass_w(1)
    pass_w(2)
    z_got(0, 1, 0)
    z_got(1, 1, 0)
    pass_w(3)
    z_got(0, 0, 1)
    z_got(1, 0, 1)
    have_w(0)
    add_up(0, 0, 0, 0)
    pass_w(4)
    pass_w(5)
    add_up(0, 1, 0, 1)
    pass_w(6)
    z_got(0, 0, 2)
    z_got(1, 0, 2)
    have_w(1)
    add_up(1, 0, 1, 1)
    z_got(0, 0, 3)
    z_got(1, 0, 3)
    z_got(0, 2, 0)
    z_got(1, 2, 0)
    for k in range(KB // 128):
        locals_[5 + k].wait()
    low_part(0, 1)
    have_w(2)
    add_up(2, 1, 1, 0)
    add_up(1, 0, 1, 0)
    z_got(0, 1, 1)
    z_got(1, 1, 1)
    add_up(2, 1, 1, 1)
    z_got(0, 1, 2)
    z_got(1, 1, 2)
    have_w(3)
    z_got(0, 1, 3)
    z_got(1, 1, 3)
    low_part(7, 2)
    add_up(3, 0, 2, 1)
    have_w(4)
    add_up(4, 1, 2, 0)
    z_got(0, 3, 0)
    z_got(1, 2, 1)
    z_got(0, 2, 1)
    z_got(1, 2, 2)
    add_up(3, 0, 2, 0)
    have_w(5)
    z_got(0, 2, 2)
    z_got(1, 2, 3)
    z_got(0, 2, 3)
    low_part(6, 3)
    add_up(4, 1, 2, 1)
    have_w(6)
    add_up(5, 0, 3, 1)
    z_got(0, 3, 1)
    z_got(1, 3, 2)
    add_up(6, 1, 3, 0)
    z_got(1, 3, 3)
    low_part(5, 4)
    low_codes()
    add_up(5, 0, 3, 0)
    add_up(6, 1, 3, 1)
    low_total()
    all_parts()
    for d in range(1, NY):
        lg(d).wait_recv()
    start(lh())
    locals_[2].wait()
    finish(c)
    lh().wait_recv()
    finish(1 - c)
    drain(sent)


def body(features, key_value_weight, adapter_down_factors, adapter_up_factors, row_adapter_index, ranks):
    down = adapter_down_factors.transpose(1, 2, 0).reshape(NZ, 16, NY * KB)
    up = adapter_up_factors.reshape(ADAPTERS * RANK, COLS)
    index = row_adapter_index.reshape(ROWS // 128, 128)
    vmem, any_ = pl.BlockSpec(memory_space=pltpu.VMEM), pl.BlockSpec(memory_space=pl.ANY)
    bf16, f32 = jnp.bfloat16, jnp.float32
    dma = pltpu.SemaphoreType.DMA
    return pl.pallas_call(
        kernel,
        out_shape=jax.ShapeDtypeStruct((NY, 2, LOWROWS, COLS), bf16),
        in_specs=[any_] * 6,
        out_specs=vmem,
        scratch_shapes=[
            pltpu.VMEM((ROWS, KB), bf16),
            pltpu.VMEM((NY - 1, KB, COLS), bf16),
            pltpu.VMEM((KB, COLS), bf16),
            pltpu.VMEM((KB // 128, NZ, NY * 16, 128), bf16),
            pltpu.VMEM((ADAPTERS * RANK, COLS), bf16),
            pltpu.VMEM((ROWS // 128, 128), jnp.int32),
            pltpu.SMEM((ADAPTERS,), jnp.int32),
            pltpu.VMEM((2, 4, ROWS, COLS), bf16),
            pltpu.VMEM((2, HALF, COLS), f32),
            pltpu.VMEM((2, 4, ROWS, COLS), bf16),
            pltpu.VMEM((2, HALF, COLS), f32),
            pltpu.VMEM((NY, 2, LOWROWS, 128), jnp.int32),
            pltpu.VMEM((NY, 2, LOWROWS, 128), f32),
            pltpu.VMEM((ROWS, 128), f32),
            pltpu.VMEM((NY, 2, PAIR, 128), bf16),
            pltpu.VMEM((NT, PAIR, 128), bf16),
            pltpu.VMEM((NY, 2, LOWROWS, 128), bf16),
            pltpu.VMEM((NY, 2, LOWROWS, COLS), f32),
            dma((5 + KB // 128,)),
            dma((2,)),
            dma((2, 7)),
            dma((2, 7, 3)),
            dma((2, 7, 2)),
            dma((2, 3)),
            dma((2, 2, 4, 4)),
            dma((2, 2, 4, 2)),
            dma((2, NT)),
            dma((2, NY)),
            dma((2,)),
        ],
        compiler_params=pltpu.CompilerParams(
            collective_id=0, has_side_effects=True, vmem_limit_bytes=60 << 20
        ),
        cost_estimate=pl.CostEstimate(
            flops=2 * ROWS * KB * 2048 + 2 * ROWS * 2048 * COLS,
            bytes_accessed=8 << 20,
            transcendentals=0,
        ),
    )(features, key_value_weight, down, up, index, ranks).reshape(ROWS, COLS)


def solution(mesh):
    in_specs = (
        P("dp", "tensor"),
        P(None, "tensor"),
        P(None, None, "tensor"),
        P(None, None, "tensor"),
        P("dp"),
        P(),
    )
    out_specs = P("dp", "tensor")
    return jax.shard_map(body, mesh=mesh, in_specs=in_specs, out_specs=out_specs, check_vma=False)
```

```python
import functools

import jax
import jax.numpy as jnp
from jax import lax
from jax.experimental import pallas as pl
from jax.experimental.pallas import tpu as pltpu
from jax.sharding import PartitionSpec as P

MESH = pl.DeviceIdType.MESH
NX, NY, NZ, NT = 4, 8, 8, 16
ROWS = 1024
HALF = ROWS // 2
KB = 1024
KX = KB // NX
COLS = 128
ADAPTERS, RANK = 16, 128
LOWROWS = ROWS // NT
PAIR = LOWROWS // 2
TILE = 512

OFFSETS = (4, 3, -3, 2, -2, 1, -1)
UP, DOWN = (0, 1, 3, 5), (0, 2, 4, 6)
LONG = (0, 1)
X_HOPS = (1, -1, 2)


def mod(value, size):
    return lax.rem(value + size, size)


def kernel(
    feat_hbm,
    weight_hbm,
    down_hbm,
    up_hbm,
    index_hbm,
    ranks_hbm,
    out_ref,
    feat,
    weight,
    own_weight,
    down,
    up,
    index_ref,
    ranks_ref,
    send16,
    send32,
    recv16,
    recv32,
    row_adapter,
    row_rank,
    low_sum,
    low_send,
    low_recv,
    low,
    base,
    local_sem,
    feat_sem,
    wy_sem,
    wx_sem,
    dy_sem,
    dx_sem,
    dz_sem,
    sum_sem,
    lr_sem,
    lg_sem,
    lh_sem,
):
    g, t = lax.axis_index("dp"), lax.axis_index("tensor")
    z, x = lax.div(g, NX), lax.rem(g, NX)
    y, c = lax.div(t, 2), lax.rem(t, 2)

    def at(dz=0, dx=0, dy=0):
        return (mod(z + dz, NZ) * NX + mod(x + dx, NX), mod(y + dy, NY) * 2 + c)

    def line(n):
        return (g, mod(y + n // 2, NY) * 2 + (c if n % 2 == 0 else 1 - c))

    sibling = line(1)

    barrier = pltpu.get_barrier_semaphore()
    for n in range(1, NT):
        pl.semaphore_signal(barrier, inc=1, device_id=line(n), device_id_type=MESH)
    for d in X_HOPS:
        pl.semaphore_signal(barrier, inc=1, device_id=at(dx=d), device_id_type=MESH)
    for d in (1, -1):
        pl.semaphore_signal(barrier, inc=1, device_id=at(dz=d), device_id_type=MESH)

    def local(n, src, dst):
        return pltpu.make_async_copy(src, dst, local_sem.at[n])

    def remote(src, dst, sems, n, device):
        return pltpu.make_async_remote_copy(
            src_ref=src,
            dst_ref=dst,
            send_sem=sems.at[(0, *n)],
            recv_sem=sems.at[(1, *n)],
            device_id=device,
            device_id_type=MESH,
        )

    my_k = pl.ds(pl.multiple_of(x * KX, KX), KX)
    half_k = pl.ds(pl.multiple_of(c * (KB // 2), KB // 2), KB // 2)
    chip_k = pl.ds(pl.multiple_of(y * KB, KB), KB)

    def down_k(chip, k):
        return pl.ds(pl.multiple_of(chip * KB + k * 128, 128), 128)

    own_rows, other_rows = pl.ds(0, 16), pl.ds(16, NY * 16 - 16)
    locals_ = [
        local(0, feat_hbm, feat.at[:, half_k]),
        local(1, weight_hbm.at[chip_k, :], own_weight),
        local(2, up_hbm, up),
        local(3, index_hbm, index_ref),
        local(4, ranks_hbm, ranks_ref),
        *[
            local(5 + k, down_hbm.at[:, :, down_k(y, k)], down.at[k, :, own_rows])
            for k in range(KB // 128)
        ],
    ]
    for copy in locals_[3:5]:
        copy.start()

    pl.semaphore_wait(barrier, NT - 1 + len(X_HOPS) + 2)

    feat_copy = remote(feat_hbm, feat.at[:, half_k], feat_sem, (), sibling)

    def wy(i):
        to = mod(y - OFFSETS[i], NY)
        src = weight_hbm.at[pl.ds(pl.multiple_of(to * KB + x * KX, KX), KX), :]
        return remote(src, weight.at[i, my_k, :], wy_sem, (i,), at(dy=-OFFSETS[i]))

    def wx(i, n):
        part = weight.at[i, my_k, :]
        return remote(part, part, wx_sem, (i, n), at(dx=X_HOPS[n]))

    def dy(i, h):
        to = mod(y - OFFSETS[i], NY)
        src = down_hbm.at[z, :, down_k(to, 2 * x + h)]
        dst = down.at[2 * x + h, z, pl.ds(OFFSETS[i] % NY * 16, 16)]
        return remote(src, dst, dy_sem, (i, h), at(dy=-OFFSETS[i]))

    def dx(n):
        part = down.at[pl.ds(2 * x, 2), z, other_rows]
        return remote(part, part, dx_sem, (n,), at(dx=X_HOPS[n]))

    def dz(way, hop, part):
        sign = 1 - 2 * way
        of = mod(x + (0, -1, 1, 2)[part], NX)
        ref = down.at[pl.ds(2 * of, 2), mod(z - sign * hop, NZ), other_rows]
        return remote(ref, ref, dz_sem, (way, hop, part), at(dz=sign))

    def rs(way, step, half):
        if step == 3 and half == LONG[way]:
            src, dst = send32.at[way], recv32.at[way]
        else:
            rows = pl.ds(half * HALF, HALF)
            src, dst = send16.at[way, step, rows], recv16.at[way, step, rows]
        return remote(src, dst, sum_sem, (way, step, half), at(dy=1 - 2 * way))

    def lr(n):
        to = mod(y + n // 2, NY), c if n % 2 == 0 else 1 - c
        return remote(low_send.at[to], low_recv.at[n], lr_sem, (n,), line(n))

    def lg(d):
        part = low.at[y, c]
        return remote(part, part, lg_sem, (d,), at(dy=d))

    def lh():
        part = low.at[:, c]
        return remote(part, part, lh_sem, (), sibling)

    sent, late, codes = [], [], []

    def start(copy, among=sent):
        copy.start()
        among.append(copy)

    def drain(copies):
        for copy in copies:
            copy.wait_send()
        copies.clear()

    def pass_w(i):
        wy(i).wait_recv()
        for n in (2, 0, 1):
            start(wx(i, n))

    def have_w(i):
        for n in range(3):
            wx(i, n).wait_recv()

    def add_up(i, way, step, half):
        before = step >= 2 or (step == 1 and half == LONG[way])
        if before:
            rs(way, step - 1, half).wait_recv()

        @pl.loop(0, HALF // TILE)
        def _(n):
            rows = pl.ds(pl.multiple_of(half * HALF + n * TILE, TILE), TILE)
            part = jnp.dot(feat[rows, :], weight[i], preferred_element_type=jnp.float32)
            if before:
                part = part + recv16[way, step - 1, rows, :].astype(jnp.float32)
            if step == 3 and half == LONG[way]:
                send32[way, pl.ds(pl.multiple_of(n * TILE, TILE), TILE), :] = part
            else:
                send16[way, step, rows, :] = part.astype(jnp.bfloat16)

        start(rs(way, step, half), late if step == 3 else sent)

    lane = lax.broadcasted_iota(jnp.int32, (TILE, 128), 1)
    lane_pair = lax.rem(lax.div(lane, 8), 2)
    pair_lane = lax.rem(
        lax.div(lax.broadcasted_iota(jnp.int32, (2, PAIR, 128), 2), 8), 2
    )

    def tile_of(ref, n):
        return ref[pl.ds(n * (TILE // 128), TILE // 128)].reshape(TILE, 128)

    def low_part(back, other_back):
        first, second = mod(z - back, NZ), mod(z - other_back, NZ)
        factors = jnp.concatenate(
            [
                jnp.concatenate([down[k, source] for k in range(KB // 128)], axis=1)
                for source in (first, second)
            ],
            axis=0,
        )

        @pl.loop(0, ROWS // TILE)
        def _(n):
            rows = pl.ds(pl.multiple_of(n * TILE, TILE), TILE)
            part = lax.dot_general(
                feat[rows, :],
                factors,
                (((1,), (1,)), ((), ())),
                preferred_element_type=jnp.float32,
            )
            ids = tile_of(row_adapter, n)
            total = low_sum[rows, :]
            for source, columns in ((first, part[:, :128]), (second, part[:, 128:])):
                total = jnp.where(ids == 2 * source + lane_pair, columns, total)
            low_sum[rows, :] = total

    def z_got(way, hop, part):
        dz(way, hop, part).wait_recv()
        if hop < 2 or (hop == 2 and part in ((0, 1), (2, 3))[way]):
            start(dz(way, hop + 1, part))

    def low_codes():
        position = lax.div(lane, 16) * 16 + c * 8 + lax.rem(lane, 8)
        for d in (4, 3, 5, 2, 6, 1, 7, 0):
            chip = mod(y + d, NY)
            rows = pl.ds(pl.multiple_of(chip * 128, 128), 128)
            mine = pltpu.roll(low_sum[rows, :], 16 * y, 1)
            kept = position[:128].astype(jnp.float32) < row_rank[chip].reshape(128, 128)
            mine = jnp.where(kept, mine, 0.0)
            left, right = pltpu.roll(mine, 120, 1), pltpu.roll(mine, 8, 1)
            both = mine + jnp.where(lane_pair[:128] == 0, left, right)
            both = both.reshape(2, 2, PAIR, 128)
            pair = jnp.where(pair_lane == 0, both[:, 0], both[:, 1])
            low_send[chip] = pair.astype(jnp.bfloat16)
            for n in (2 * d, 2 * d + 1):
                if n:
                    start(lr(n), codes)
        drain(sent)

    def low_total():
        totals = [low_send[y, c].astype(jnp.float32), None]
        for n in range(1, NT):
            lr(n).wait_recv()
        for n in range(1, NT):
            part = low_recv[n].astype(jnp.float32)
            totals[n % 2] = part if totals[n % 2] is None else totals[n % 2] + part
        even = jnp.where(c == 0, totals[0], totals[1])
        odd = jnp.where(c == 0, totals[1], totals[0])
        first = jnp.where(lane_pair[:PAIR] == 0, even, pltpu.roll(odd, 8, 1))
        second = jnp.where(lane_pair[:PAIR] == 0, pltpu.roll(even, 120, 1), odd)
        low[y, c, :PAIR] = first.astype(jnp.bfloat16)
        low[y, c, PAIR:] = second.astype(jnp.bfloat16)
        for d in range(1, NY):
            start(lg(d))
        drain(codes)

    def own_part():
        locals_[1].wait()

        @pl.loop(0, ROWS // TILE)
        def _(n):
            rows = pl.ds(pl.multiple_of(n * TILE, TILE), TILE)
            part = jnp.dot(feat[rows, :], own_weight[...], preferred_element_type=jnp.float32)
            base[pl.ds(n * (TILE // 128), TILE // 128)] = part.reshape(TILE // 128, 2, LOWROWS, 128)

    def all_parts():
        for way in range(2):
            for half in range(2):
                rs(way, 3, half).wait_recv()
        for half in range(2):
            rows = slice(half * HALF, (half + 1) * HALF)
            chips = slice(half * NY // 2, (half + 1) * NY // 2)
            total = base[chips]
            for way in range(2):
                if half == LONG[way]:
                    total += recv32[way].reshape(total.shape)
                else:
                    total += recv16[way, 3, rows, :].astype(jnp.float32).reshape(total.shape)
            base[chips] = total
        drain(late)

    def finish(core):
        @pl.loop(0, NY * LOWROWS // TILE)
        def _(n):
            group = (pl.ds(n * (TILE // LOWROWS), TILE // LOWROWS), core)
            code = low[group].reshape(TILE, 128).astype(jnp.float32)
            ids = row_adapter[group].reshape(TILE, 128)
            spread = [
                jnp.where(ids == a, code, 0.0).astype(jnp.bfloat16) for a in range(ADAPTERS)
            ]
            update = jnp.dot(
                jnp.concatenate(spread, axis=1), up[...], preferred_element_type=jnp.float32
            )
            scale = 4.0 / jnp.sqrt(row_rank[group])
            total = base[group] + scale * update.reshape(scale.shape)
            out_ref[group] = total.astype(jnp.bfloat16)

    for i in range(7):
        for h in range(2):
            start(dy(i, h))
    for i in range(7):
        start(wy(i))
    start(feat_copy)
    for copy in locals_[:3] + locals_[5:]:
        copy.start()
    locals_[3].wait()
    locals_[4].wait()
    for r in range(ROWS // 128):
        ids = index_ref[r : r + 1, :].astype(jnp.float32)
        spread = jnp.transpose(jnp.broadcast_to(ids, (128, 128)))
        row_adapter[r] = spread.astype(jnp.int32).reshape(2, LOWROWS, 128)

    @pl.loop(0, ROWS // 128)
    def _(r):
        ids = row_adapter[r]
        rank = jnp.zeros((2, LOWROWS, 128), jnp.float32)
        for a in range(ADAPTERS):
            rank = jnp.where(ids == a, ranks_ref[a].astype(jnp.float32), rank)
        row_rank[r] = rank

    low_sum[...] = jnp.zeros_like(low_sum)
    for i in range(7):
        for h in range(2):
            dy(i, h).wait_recv()
    for n in (2, 0, 1):
        start(dx(n))
    for way in range(2):
        start(dz(way, 0, 0))
    locals_[0].wait()
    feat_copy.wait_recv()
    own_part()
    pass_w(0)
    z_got(0, 0, 0)
    z_got(1, 0, 0)
    for n in range(3):
        dx(n).wait_recv()
    for part in (1, 2, 3):
        for way in range(2):
            start(dz(way, 0, part))
    pass_w(1)
    pass_w(2)
    z_got(0, 1, 0)
    z_got(1, 1, 0)
    pass_w(3)
    z_got(0, 0, 1)
    z_got(1, 0, 1)
    have_w(0)
    add_up(0, 0, 0, 0)
    pass_w(4)
    pass_w(5)
    add_up(0, 1, 0, 1)
    pass_w(6)
    z_got(0, 0, 2)
    z_got(1, 0, 2)
    have_w(1)
    add_up(1, 0, 1, 1)
    z_got(0, 0, 3)
    z_got(1, 0, 3)
    z_got(0, 2, 0)
    z_got(1, 2, 0)
    for k in range(KB // 128):
        locals_[5 + k].wait()
    low_part(0, 1)
    have_w(2)
    add_up(2, 1, 1, 0)
    add_up(1, 0, 1, 0)
    z_got(0, 1, 1)
    z_got(1, 1, 1)
    add_up(2, 1, 1, 1)
    z_got(0, 1, 2)
    z_got(1, 1, 2)
    have_w(3)
    z_got(0, 1, 3)
    z_got(1, 1, 3)
    low_part(7, 2)
    add_up(3, 0, 2, 1)
    have_w(4)
    add_up(4, 1, 2, 0)
    z_got(0, 3, 0)
    z_got(1, 2, 1)
    z_got(0, 2, 1)
    z_got(1, 2, 2)
    add_up(3, 0, 2, 0)
    have_w(5)
    z_got(0, 2, 2)
    z_got(1, 2, 3)
    z_got(0, 2, 3)
    low_part(6, 3)
    add_up(4, 1, 2, 1)
    have_w(6)
    add_up(5, 0, 3, 1)
    z_got(0, 3, 1)
    z_got(1, 3, 2)
    add_up(6, 1, 3, 0)
    z_got(1, 3, 3)
    low_part(5, 4)
    low_codes()
    add_up(5, 0, 3, 0)
    add_up(6, 1, 3, 1)
    low_total()
    all_parts()
    for d in range(1, NY):
        lg(d).wait_recv()
    start(lh())
    locals_[2].wait()
    finish(c)
    lh().wait_recv()
    finish(1 - c)
    drain(sent)


def body(features, key_value_weight, adapter_down_factors, adapter_up_factors, row_adapter_index, ranks):
    down = adapter_down_factors.transpose(1, 2, 0).reshape(NZ, 16, NY * KB)
    up = adapter_up_factors.reshape(ADAPTERS * RANK, COLS)
    index = row_adapter_index.reshape(ROWS // 128, 128)
    vmem, any_ = pl.BlockSpec(memory_space=pltpu.VMEM), pl.BlockSpec(memory_space=pl.ANY)
    bf16, f32 = jnp.bfloat16, jnp.float32
    dma = pltpu.SemaphoreType.DMA
    return pl.pallas_call(
        kernel,
        out_shape=jax.ShapeDtypeStruct((NY, 2, LOWROWS, COLS), bf16),
        in_specs=[any_] * 6,
        out_specs=vmem,
        scratch_shapes=[
            pltpu.VMEM((ROWS, KB), bf16),
            pltpu.VMEM((NY - 1, KB, COLS), bf16),
            pltpu.VMEM((KB, COLS), bf16),
            pltpu.VMEM((KB // 128, NZ, NY * 16, 128), bf16),
            pltpu.VMEM((ADAPTERS * RANK, COLS), bf16),
            pltpu.VMEM((ROWS // 128, 128), jnp.int32),
            pltpu.SMEM((ADAPTERS,), jnp.int32),
            pltpu.VMEM((2, 4, ROWS, COLS), bf16),
            pltpu.VMEM((2, HALF, COLS), f32),
            pltpu.VMEM((2, 4, ROWS, COLS), bf16),
            pltpu.VMEM((2, HALF, COLS), f32),
            pltpu.VMEM((NY, 2, LOWROWS, 128), jnp.int32),
            pltpu.VMEM((NY, 2, LOWROWS, 128), f32),
            pltpu.VMEM((ROWS, 128), f32),
            pltpu.VMEM((NY, 2, PAIR, 128), bf16),
            pltpu.VMEM((NT, PAIR, 128), bf16),
            pltpu.VMEM((NY, 2, LOWROWS, 128), bf16),
            pltpu.VMEM((NY, 2, LOWROWS, COLS), f32),
            dma((5 + KB // 128,)),
            dma((2,)),
            dma((2, 7)),
            dma((2, 7, 3)),
            dma((2, 7, 2)),
            dma((2, 3)),
            dma((2, 2, 4, 4)),
            dma((2, 2, 4, 2)),
            dma((2, NT)),
            dma((2, NY)),
            dma((2,)),
        ],
        compiler_params=pltpu.CompilerParams(
            collective_id=0, has_side_effects=True, vmem_limit_bytes=60 << 20
        ),
        cost_estimate=pl.CostEstimate(
            flops=2 * ROWS * KB * 2048 + 2 * ROWS * 2048 * COLS,
            bytes_accessed=8 << 20,
            transcendentals=0,
        ),
    )(features, key_value_weight, down, up, index, ranks).reshape(ROWS, COLS)


def solution(mesh):
    in_specs = (
        P("dp", "tensor"),
        P(None, "tensor"),
        P(None, None, "tensor"),
        P(None, None, "tensor"),
        P("dp"),
        P(),
    )
    out_specs = P("dp", "tensor")
    return jax.shard_map(body, mesh=mesh, in_specs=in_specs, out_specs=out_specs, check_vma=False)
```
